32 devices in a mesh: slab: 16 (over z, y, core), angle: 2 (over x).
Axes of the slice: x: 2, y: 2, z: 4, core: 2. Of those that a mesh axis runs over, the one named last changes fastest.
Arguments:
- object_density: bfloat16 [2, 128, 32, 320], P(None, 'slab', 'angle'), may hold values from -6 to 6
- resampling_matrices: bfloat16 [2, 64, 128], replicated, may hold values from -0.109375 to 0.109375
- receiving_tile_number: int32 [2, 16, 2], replicated, may hold values from 0 to 4
- illumination_modes: bfloat16 [4, 2, 256, 256], replicated, may hold values from -3 to 3
- window_corners: int32 [2, 16, 2], P('angle', 'slab'), may hold values from 1 to 63
- observed_power: float32 [2, 16, 256, 256], P('angle', 'slab'), may hold values from 0.5 to 2
Outputs:
- vol_grad: float32 [2, 128, 32, 320], P(None, 'slab', 'angle')
- probe_grad: float32 [4, 2, 256, 256], P(None, None, 'slab')
- power_mismatch: float32 [2, 16, 256, 256], P('angle', 'slab')
- locus_derivative: float32 [2, 16, 2], P('angle', 'slab')
The draws below stay inside these ranges and needn't reach their ends.
All inputs are finite; a program needn't handle non-finite values.
Results may differ from the reference program's by a relative error of at most 0.00035.
Values sent between devices are 32-bit elements; how exact they have to be, the bound alone decides.
A program may use at most 64 MiB of HBM per device.

```python
import jax
import jax.numpy as jnp
from jax import lax

BEAM_WIDTH_PIX = 256
MODES = 4
UB = 64
NUB = 5
NZ = 320
TY = 16
CX = 8
TILES_DEV = 1
NUM_VIEWS = 2
NX = 128
NY = 32
NUM_FOCI = 16
N_SLAB = 16
N_ANGLE = 2


def place_ends(values, own_key, smallest, high):
    place = [jax.random.randint(jax.random.fold_in(own_key, axis), (), 0, length) for axis, length in enumerate(values.shape)]
    longest = values.shape.index(max(values.shape))
    beside = place[:longest] + [(place[longest] + 1) % values.shape[longest]] + place[longest + 1:]
    return values.at[tuple(place)].set(smallest).at[tuple(beside)].set(high)


def steps_of(own_key, extent, pieces, smallest, top_value):
    def one(position, parts):
        heights = jax.random.uniform(jax.random.fold_in(jax.random.fold_in(own_key, 6), position), (parts,), jnp.float32, smallest / len(pieces), top_value / len(pieces))
        return jnp.repeat(jnp.exp(heights), extent[position] // parts).reshape((-1,) + (1,) * (len(extent) - position - 1))

    loudness = one(*pieces[0])
    for cut in pieces[1:]:
        loudness = loudness * one(*cut)
    return loudness


def normal_values(key, extent, spread, most, split=(), kind=jnp.bfloat16):
    loudness = steps_of(key, extent, split, -0.22, 0.18) if split else 1.0
    result = jax.random.normal(key, extent, jnp.float32) * spread * loudness
    return jnp.minimum(jnp.maximum(result, -most), most).astype(kind)


def setup_inputs(seed: int = 0) -> dict:
    keys = jax.random.split(jax.random.key(seed), 7)
    object_density = normal_values(keys[0], (2, NX, NY, NZ), 1.0, 6.0, ((1, 16), (2, 2)))
    resampling_matrices = normal_values(keys[1], (NUM_VIEWS, UB, CX * TY), (4 * NX * NY // NUB) ** -0.5, 0.109375)
    receiving_tile_number = place_ends(jax.random.randint(keys[2], (NUM_VIEWS, N_SLAB, TILES_DEV * N_ANGLE), 0, NUB), jax.random.fold_in(keys[2], 1), 0, NUB - 1).astype(jnp.int32)
    illumination_modes = normal_values(keys[3], (MODES, 2, BEAM_WIDTH_PIX, BEAM_WIDTH_PIX), 0.5, 3.0)
    window_corners = place_ends(jax.random.randint(keys[4], (NUM_VIEWS, NUM_FOCI, 2), 1, min(UB * NUB, NZ) - BEAM_WIDTH_PIX), jax.random.fold_in(keys[4], 1), 1, (min(UB * NUB, NZ) - BEAM_WIDTH_PIX) - 1).astype(jnp.int32)
    observed_power = jnp.clip(0.5 + 1.5 * jax.random.uniform(keys[5], (NUM_VIEWS, NUM_FOCI, BEAM_WIDTH_PIX, BEAM_WIDTH_PIX), jnp.float32) ** steps_of(keys[5], (NUM_VIEWS, NUM_FOCI, BEAM_WIDTH_PIX, BEAM_WIDTH_PIX), ((0, 2), (1, 16)), -0.2, 0.2), 0.5, 2.0)
    return {"object_density": object_density, "resampling_matrices": resampling_matrices, "receiving_tile_number": receiving_tile_number, "illumination_modes": illumination_modes, "window_corners": window_corners, "observed_power": observed_power}


def spot_loss(patch, illumination_modes, recorded_diffraction):
    absorb = jnp.exp(-patch[1])
    t_real = absorb * jnp.cos(patch[0])
    t_imag = absorb * jnp.sin(patch[0])
    e_real = illumination_modes[:, 0] * t_real - illumination_modes[:, 1] * t_imag
    e_imag = illumination_modes[:, 0] * t_imag + illumination_modes[:, 1] * t_real
    field = jnp.fft.fft2(e_real + 1j * e_imag, axes=(1, 2), norm='ortho')
    inten = lax.optimization_barrier(jnp.sum(jnp.real(field) ** 2 + jnp.imag(field) ** 2, axis=0))
    resid = inten - recorded_diffraction
    return (0.5 * jnp.sum(resid * resid), resid)

def reference(object_density, resampling_matrices, receiving_tile_number, illumination_modes, window_corners, observed_power):
    highest = lax.Precision.HIGHEST
    x_tiles = NX // CX
    y_tiles = NY // TY
    tiles = object_density.astype(jnp.float32).reshape(2, x_tiles, CX, y_tiles, TY, NZ)
    tiles = tiles.transpose(1, 3, 0, 2, 4, 5).reshape(x_tiles * y_tiles, 2, CX * TY, NZ)
    kernel_f = resampling_matrices.astype(jnp.float32)

    def project(angle_id):
        summed = jax.ops.segment_sum(tiles, receiving_tile_number[angle_id].reshape(-1), num_segments=NUB)
        return jnp.einsum('uk,dckz->cduz', kernel_f[angle_id], summed, precision=highest).reshape(2, NUB * UB, NZ)
    sinogram_views = lax.map(project, jnp.arange(NUM_VIEWS, dtype=jnp.int32))
    probe_f = illumination_modes.astype(jnp.float32)

    def foci_per_view(input_arrays):
        projection_at_angle, offsets_at_angle, measured_at_angle = input_arrays

        def single_spot(carry, items):
            blank_detector, probe_gradient_total = carry
            offset, recorded_diffraction = items
            col_off = offset[0].astype(jnp.int32)
            row_off = offset[1].astype(jnp.int32)
            window = lax.dynamic_slice(projection_at_angle, (jnp.int32(0), col_off - 1, row_off - 1), (2, BEAM_WIDTH_PIX + 2, BEAM_WIDTH_PIX + 2))
            patch = window[:, 1:-1, 1:-1]
            loss, pull, resid = jax.vjp(lambda patch_in, probe_in: spot_loss(patch_in, probe_in, recorded_diffraction), patch, probe_f, has_aux=True)
            patch_grad, probe_term = pull(jnp.ones((), loss.dtype))
            current = lax.dynamic_slice(blank_detector, (jnp.int32(0), col_off, row_off), (2, BEAM_WIDTH_PIX, BEAM_WIDTH_PIX))
            blank_detector = lax.dynamic_update_slice(blank_detector, current + patch_grad, (jnp.int32(0), col_off, row_off))
            shift_col = jnp.sum(patch_grad * (window[:, 2:, 1:-1] - window[:, :-2, 1:-1])) * 0.5 / BEAM_WIDTH_PIX
            shift_row = jnp.sum(patch_grad * (window[:, 1:-1, 2:] - window[:, 1:-1, :-2])) * 0.5 / BEAM_WIDTH_PIX
            return ((blank_detector, probe_gradient_total + probe_term), (resid, jnp.stack([shift_col, shift_row])))
        start_offset = (jnp.zeros((2, NUB * UB, NZ), jnp.float32), jnp.zeros_like(probe_f))
        (blank_detector, probe_gradient_total), (residual_list, scan_shifts) = lax.scan(single_spot, start_offset, (offsets_at_angle, measured_at_angle))
        return (blank_detector, probe_gradient_total, residual_list, scan_shifts)
    sinogram_derivative, illumination_derivative_parts, power_mismatch, locus_derivative = lax.map(foci_per_view, (sinogram_views, window_corners, observed_power))
    probe_grad = lax.optimization_barrier(jnp.sum(illumination_derivative_parts, axis=0))

    def back(carry, angle_id):
        blocks = jnp.einsum('uk,cduz->dckz', kernel_f[angle_id], sinogram_derivative[angle_id].reshape(2, NUB, UB, NZ), precision=highest)
        return (carry + blocks[receiving_tile_number[angle_id].reshape(-1)], None)
    start_offset = jnp.zeros((x_tiles * y_tiles, 2, CX * TY, NZ), jnp.float32)
    tile_grad, unused = lax.scan(back, start_offset, jnp.arange(NUM_VIEWS, dtype=jnp.int32))
    vol_grad = tile_grad.reshape(x_tiles, y_tiles, 2, CX, TY, NZ).transpose(2, 0, 3, 1, 4, 5).reshape(2, NX, NY, NZ)
    return (vol_grad, probe_grad, power_mismatch, locus_derivative)
```

```python
import functools
import math

import jax
import jax.numpy as jnp
import numpy as np
from jax import lax
from jax.experimental import pallas as pl
from jax.experimental.pallas import tpu as pltpu
from jax.sharding import PartitionSpec as P

NUB = 5
INNER = 2
MID = 2
MESH = pl.DeviceIdType.MESH
VMEM = pl.BlockSpec(memory_space=pltpu.VMEM)
SMEM = pl.BlockSpec(memory_space=pltpu.SMEM)
VMEM_BYTES = 48 * 1024 * 1024


def remote(src, dst, send, recv, axis, peer):
    return pltpu.make_async_remote_copy(
        src_ref=src, dst_ref=dst, send_sem=send, recv_sem=recv,
        device_id={axis: peer}, device_id_type=MESH,
    )


def greet(n_slab, n_angle, me_s, me_a):
    barrier = pltpu.get_barrier_semaphore()
    for off in range(1, n_angle):
        pl.semaphore_signal(barrier, inc=1, device_id={"angle": lax.rem(me_a + off, n_angle)}, device_id_type=MESH)

    @pl.loop(1, n_slab)
    def _(off):
        pl.semaphore_signal(barrier, inc=1, device_id={"slab": lax.rem(me_s + off, n_slab)}, device_id_type=MESH)

    pl.semaphore_wait(barrier, n_slab + n_angle - 2)


def gather_kernel(n_slab, n_angle, blocks, hot, out, got, xbuf, xs, xr, as_, ar, zs, zr, ys, yr, cs, cr):
    n_out = n_slab // (MID * INNER)
    me_s, me_a = lax.axis_index("slab"), lax.axis_index("angle")
    me_z, me_y, me_c = me_s // (MID * INNER), lax.rem(me_s // INNER, MID), lax.rem(me_s, INNER)
    greet(n_slab, n_angle, me_s, me_a)

    def xcopy(off):
        peer = lax.rem(me_a + off, n_angle)
        return remote(blocks.at[peer], xbuf.at[off], xs.at[off], xr.at[off], "angle", peer)

    def acopy(step, off):
        peer = lax.rem(me_s + off, n_slab)
        src = blocks.at[me_a, peer] if step == 0 else xbuf.at[step, peer]
        source = lax.rem(me_a + n_angle - step, n_angle)
        return remote(src, got.at[source, me_s], as_.at[step, off], ar.at[step, off], "slab", peer)

    for off in range(1, n_angle):
        xcopy(off).start()

    @pl.loop(1, n_slab)
    def _(off):
        acopy(0, off).start()

    got[me_a, me_s] = blocks[me_a, me_s]
    for step in range(1, n_angle):
        xcopy(step).wait_recv()

        @pl.loop(1, n_slab)
        def _(off):
            acopy(step, off).start()

        got[lax.rem(me_a + n_angle - step, n_angle), me_s] = xbuf[step, me_s]
    for step in range(n_angle):

        @pl.loop(1, n_slab)
        def _(off):
            acopy(step, off).wait_recv()

    rows, z_cells = blocks.shape[2], blocks.shape[3]

    def add(i, acc):
        for j in range(n_angle):
            item = got[j, i]
            acc = tuple(acc[d] + hot[(i * n_angle + j) * NUB + d] * item for d in range(NUB))
        return acc

    acc = lax.fori_loop(0, n_slab, add, tuple(jnp.zeros((rows, z_cells), jnp.float32) for _ in range(NUB)))
    for d in range(NUB):
        out[me_z, me_y, me_c, d] = acc[d]

    def to_slab(z, y, c):
        return (z * MID + y) * INNER + c

    def zcopy(off):
        piece = out.at[me_z, me_y, me_c]
        return remote(piece, piece, zs.at[off], zr.at[off], "slab", to_slab(lax.rem(me_z + off, n_out), me_y, me_c))

    def ycopy(off):
        piece = out.at[lax.rem(me_z + n_out - off, n_out), me_y, me_c]
        return remote(piece, piece, ys.at[off], yr.at[off], "slab", to_slab(me_z, 1 - me_y, me_c))

    def ccopy(off, flip):
        row = 1 - me_y if flip else me_y
        piece = out.at[lax.rem(me_z + n_out - off, n_out), row, me_c]
        return remote(piece, piece, cs.at[flip, off], cr.at[flip, off], "slab", to_slab(me_z, me_y, 1 - me_c))

    ycopy(0).start()
    for off in range(1, n_out):
        zcopy(off).start()
    ccopy(0, 0).start()
    for off in range(1, n_out):
        zcopy(off).wait_recv()
        ycopy(off).start()
        ccopy(off, 0).start()
    for off in range(n_out):
        ycopy(off).wait_recv()
        ccopy(off, 1).start()
    for off in range(n_out):
        ccopy(off, 0).wait_recv()
        ccopy(off, 1).wait_recv()
        ycopy(off).wait_send()
        ccopy(off, 0).wait_send()
        ccopy(off, 1).wait_send()
    for off in range(1, n_out):
        zcopy(off).wait_send()
    for off in range(1, n_angle):
        xcopy(off).wait_send()
    for step in range(n_angle):

        @pl.loop(1, n_slab)
        def _(off):
            acopy(step, off).wait_send()


def reduce_kernel(
    n_slab, n_angle, pg, q, hot, vin, pr,
    p1, s1, p2, s2, p3, q1, t1, q2, t2, q3, t3, q4, disp, got,
    ps, pr_, pzs, pzr, ds, dr, vs, vr, qs, qr, qxs, qxr, qzs, qzr, qgs, qgr,
):
    n_out = n_slab // (MID * INNER)
    me_s, me_a = lax.axis_index("slab"), lax.axis_index("angle")
    me_z, me_y, me_c = me_s // (MID * INNER), lax.rem(me_s // INNER, MID), lax.rem(me_s, INNER)
    greet(n_slab, n_angle, me_s, me_a)
    planes = q.shape[0] // n_angle

    def to_slab(z, y, c):
        return (z * MID + y) * INNER + c

    core_peer = to_slab(me_z, me_y, 1 - me_c)
    mid_peer = to_slab(me_z, 1 - me_y, me_c)
    p_core = remote(pg.at[:, :, 1 - me_c], p1, ps.at[0], pr_.at[0], "slab", core_peer)
    p_core.start()
    q_core = remote(q.at[:, :, :, 1 - me_c], q1, qs.at[0], qr.at[0], "slab", core_peer)
    q_core.start()
    p_core.wait_recv()
    s1[...] = pg[:, :, me_c] + p1[...]
    p_mid = remote(s1.at[:, 1 - me_y], p2, ps.at[1], pr_.at[1], "slab", mid_peer)
    p_mid.start()
    q_core.wait_recv()
    t1[...] = q[:, :, :, me_c] + q1[...]

    def qx(off):
        peer = lax.rem(me_a + off, n_angle)
        return remote(t1.at[pl.ds(peer * planes, planes)], q2.at[off], qxs.at[off], qxr.at[off], "angle", peer)

    for off in range(1, n_angle):
        qx(off).start()
    p_mid.wait_recv()
    s2[...] = s1[:, me_y] + p2[...]

    def pz(off):
        z = lax.rem(me_z + off, n_out)
        return remote(s2.at[z], p3.at[off], pzs.at[off], pzr.at[off], "slab", to_slab(z, me_y, me_c))

    for off in range(1, n_out):
        pz(off).start()
    total = s2[me_z]
    for off in range(1, n_out):
        pz(off).wait_recv()
        total = total + p3[off]

    @pl.loop(0, n_slab)
    def _(i):
        for j in range(n_angle):
            base = (i * n_angle + j) * NUB
            block = hot[base] * total[0]
            for d in range(1, NUB):
                block = block + hot[base + d] * total[d]
            disp[i, j] = block

    def dcopy(off):
        peer = lax.rem(me_s + off, n_slab)
        return remote(disp.at[peer], got.at[:, me_s], ds.at[off], dr.at[off], "slab", peer)

    @pl.loop(1, n_slab)
    def _(off):
        dcopy(off).start()

    for j in range(n_angle):
        got[j, me_s] = disp[me_s, j]

    t2[...] = t1[pl.ds(me_a * planes, planes)]
    for off in range(1, n_angle):
        qx(off).wait_recv()
        t2[...] += q2[off]
    q_mid = remote(t2.at[:, :, 1 - me_y], q3, qs.at[1], qr.at[1], "slab", mid_peer)
    q_mid.start()

    @pl.loop(1, n_slab)
    def _(off):
        dcopy(off).wait_recv()

    def vx(off):
        peer = lax.rem(me_a + off, n_angle)
        return remote(got.at[peer], vin.at[me_a], vs.at[off], vr.at[off], "angle", peer)

    for off in range(1, n_angle):
        vx(off).start()
    vin[me_a] = got[me_a]
    q_mid.wait_recv()
    t3[...] = t2[:, :, me_y] + q3[...]

    def qz(off):
        z = lax.rem(me_z + off, n_out)
        return remote(t3.at[:, z], q4.at[off], qzs.at[off], qzr.at[off], "slab", to_slab(z, me_y, me_c))

    for off in range(1, n_out):
        qz(off).start()
    probe = t3[:, me_z]
    for off in range(1, n_out):
        qz(off).wait_recv()
        probe = probe + q4[off]
    mine = pl.ds(me_a * planes, planes)
    pr[mine] = probe

    def qg(off):
        return remote(pr.at[mine], pr.at[mine], qgs.at[off], qgr.at[off], "angle", lax.rem(me_a + off, n_angle))

    for off in range(1, n_angle):
        qg(off).start()
    for off in range(1, n_angle):
        qg(off).wait_recv()
        vx(off).wait_recv()
        qg(off).wait_send()
        vx(off).wait_send()
        qx(off).wait_send()
    for off in range(1, n_out):
        pz(off).wait_send()
        qz(off).wait_send()

    @pl.loop(1, n_slab)
    def _(off):
        dcopy(off).wait_send()

    p_core.wait_send()
    q_core.wait_send()
    p_mid.wait_send()
    q_mid.wait_send()


def split(x):
    high = x.astype(jnp.bfloat16)
    return high, (x - high.astype(jnp.float32)).astype(jnp.bfloat16)


def dot3(a, b):
    def dot(x, y):
        return jnp.dot(x, y, preferred_element_type=jnp.float32)

    return dot(a[0], b[0]) + (dot(a[0], b[1]) + dot(a[1], b[0]))


def spot_kernel(corner, gathered, probe, power, tabs, grad, pterm, resid_out, shift, det, trans, far, inten, tgrad):
    n_slab, _, rows, z_cells = gathered.shape
    side = probe.shape[2]
    modes = probe.shape[0]
    det_cols = det.shape[1]
    lanes = det.shape[2]
    per = n_slab // 2
    cols = per * rows
    col, row = corner[0], corner[1]
    for k in range(n_slab):
        for d in range(NUB):
            at = d * cols + (k % per) * rows
            det[k // per, at : at + rows, :z_cells] = gathered[k, d]
    for c in range(2):
        det[c, :, z_cells:] = jnp.zeros((det_cols, lanes - z_cells), jnp.float32)
        moved = pltpu.roll(det[c], lanes - row, 1)
        det[c] = pltpu.roll(moved, det_cols - col, 0)
    absorb = jnp.exp(-det[1, :side, :side])
    phase = det[0, :side, :side]
    trans[0] = absorb * jnp.cos(phase)
    trans[1] = absorb * jnp.sin(phase)
    inten[...] = -power[...]
    left = (tabs[0], tabs[1])
    right = (tabs[2], tabs[3])

    @pl.loop(0, modes)
    def _(m):
        pr_, pi_ = probe[m, 0].astype(jnp.float32), probe[m, 1].astype(jnp.float32)
        tr, ti = trans[0], trans[1]
        stacked = jnp.concatenate([pr_ * tr - pi_ * ti, pr_ * ti + pi_ * tr], axis=0)
        mid = dot3(left, split(stacked))
        both = jnp.concatenate([mid[:side], mid[side:]], axis=1)
        field = dot3(split(both), right)
        far[m] = field
        fr, fi = field[:, :side], field[:, side:]
        inten[...] += fr * fr + fi * fi

    resid_out[...] = inten[...]
    tgrad[...] = jnp.zeros_like(tgrad)

    @pl.loop(0, modes)
    def _(m):
        weight = 2.0 * inten[...]
        pull = jnp.concatenate([far[m, :, :side] * weight, far[m, :, side:] * weight], axis=0)
        mid = dot3(right, split(pull))
        both = jnp.concatenate([mid[:side], mid[side:]], axis=1)
        back = dot3(split(both), left)
        er, ei = back[:, :side], back[:, side:]
        tr, ti = trans[0], trans[1]
        pterm[m, 0] = er * tr + ei * ti
        pterm[m, 1] = ei * tr - er * ti
        pr_, pi_ = probe[m, 0].astype(jnp.float32), probe[m, 1].astype(jnp.float32)
        tgrad[0] += pr_ * er + pi_ * ei
        tgrad[1] += pr_ * ei - pi_ * er

    tr, ti = trans[0], trans[1]
    ga, gb = tgrad[0], tgrad[1]
    patch = (gb * tr - ga * ti, -(ga * tr + gb * ti))
    shift_col = jnp.float32(0.0)
    shift_row = jnp.float32(0.0)
    for c in range(2):
        here = det[c]
        dcol = pltpu.roll(here, det_cols - 1, 0)[:side, :side] - pltpu.roll(here, 1, 0)[:side, :side]
        drow = pltpu.roll(here, lanes - 1, 1)[:side, :side] - pltpu.roll(here, 1, 1)[:side, :side]
        shift_col += jnp.sum(patch[c] * dcol)
        shift_row += jnp.sum(patch[c] * drow)
    shift[0] = shift_col * 0.5 / side
    shift[1] = shift_row * 0.5 / side
    for c in range(2):
        det[c] = jnp.zeros((det_cols, lanes), jnp.float32)
        det[c, :side, :side] = patch[c]
        det[c] = pltpu.roll(pltpu.roll(det[c], row, 1), col, 0)
    for k in range(n_slab):
        for d in range(NUB):
            at = d * cols + (k % per) * rows
            grad[k, d] = det[k // per, at : at + rows, :z_cells]


def tables(length):
    ids = np.outer(np.arange(length), np.arange(length)) % length
    phases = ids * (2.0 * math.pi / length)
    c, s = np.cos(phases) / math.sqrt(length), np.sin(phases) / math.sqrt(length)
    left = np.block([[c, s], [-s, c]])
    parts = []
    for table in (left, left.T):
        high = table.astype(jnp.bfloat16)
        parts += [high, (table - high.astype(np.float64)).astype(jnp.bfloat16)]
    return jnp.asarray(np.stack(parts))


def local(object_density, resampling_matrices, receiving_tile_number, illumination_modes, window_corners, observed_power):
    n_angle = lax.axis_size("angle")
    n_slab = lax.axis_size("slab")
    n_out = n_slab // (MID * INNER)
    my_angle = lax.axis_index("angle")
    x_cells = object_density.shape[1]
    y_here = object_density.shape[2]
    z_cells = object_density.shape[3]
    tile_rows = resampling_matrices.shape[2]
    blk_cols = resampling_matrices.shape[1]
    modes, _, side, _ = illumination_modes.shape
    rows = 2 * blk_cols // n_slab
    per_slab = side // n_slab
    lanes = (z_cells + 127) // 128 * 128
    f32 = jnp.float32
    dma = pltpu.SemaphoreType.DMA

    tile = object_density.reshape(2, tile_rows, z_cells)
    blocks = jnp.einsum("auk,ckz->acuz", resampling_matrices, tile, preferred_element_type=f32)
    blocks = blocks.reshape(n_angle, n_slab, rows, z_cells)
    ids = lax.dynamic_index_in_dim(receiving_tile_number, my_angle, 0, keepdims=False).reshape(-1)
    hot = (ids[:, None] == jnp.arange(NUB, dtype=jnp.int32)[None, :]).astype(f32).reshape(-1)

    gathered = pl.pallas_call(
        functools.partial(gather_kernel, n_slab, n_angle),
        out_shape=jax.ShapeDtypeStruct((n_out, MID, INNER, NUB, rows, z_cells), f32),
        in_specs=[VMEM, SMEM],
        out_specs=VMEM,
        scratch_shapes=[
            pltpu.VMEM((n_angle, n_slab, rows, z_cells), f32),
            pltpu.VMEM((n_angle, n_slab, rows, z_cells), f32),
            dma((n_angle,)), dma((n_angle,)),
            dma((n_angle, n_slab)), dma((n_angle, n_slab)),
            dma((n_out,)), dma((n_out,)),
            dma((n_out,)), dma((n_out,)),
            dma((2, n_out)), dma((2, n_out)),
        ],
        compiler_params=pltpu.CompilerParams(collective_id=0, has_side_effects=True, vmem_limit_bytes=VMEM_BYTES),
    )(blocks, hot)

    grad, pterm, resid, shift = pl.pallas_call(
        spot_kernel,
        out_shape=(
            jax.ShapeDtypeStruct((n_slab, NUB, rows, z_cells), f32),
            jax.ShapeDtypeStruct((modes, 2, side, side), f32),
            jax.ShapeDtypeStruct((side, side), f32),
            jax.ShapeDtypeStruct((2,), f32),
        ),
        in_specs=[SMEM, VMEM, VMEM, VMEM, VMEM],
        out_specs=(VMEM, VMEM, VMEM, SMEM),
        scratch_shapes=[
            pltpu.VMEM((2, blk_cols * NUB, lanes), f32),
            pltpu.VMEM((2, side, side), f32),
            pltpu.VMEM((modes, side, 2 * side), f32),
            pltpu.VMEM((side, side), f32),
            pltpu.VMEM((2, side, side), f32),
        ],
        compiler_params=pltpu.CompilerParams(vmem_limit_bytes=VMEM_BYTES),
    )(
        window_corners.reshape(2),
        gathered.reshape(n_slab, NUB, rows, z_cells),
        illumination_modes,
        observed_power[0, 0],
        tables(side),
    )

    planes = 2 * modes // n_angle
    vin, probe_grad = pl.pallas_call(
        functools.partial(reduce_kernel, n_slab, n_angle),
        out_shape=(
            jax.ShapeDtypeStruct((n_angle, n_slab, rows, z_cells), f32),
            jax.ShapeDtypeStruct((2 * modes, per_slab, side), f32),
        ),
        in_specs=[VMEM, VMEM, SMEM],
        out_specs=(VMEM, VMEM),
        scratch_shapes=[
            pltpu.VMEM((n_out, MID, NUB, rows, z_cells), f32),
            pltpu.VMEM((n_out, MID, NUB, rows, z_cells), f32),
            pltpu.VMEM((n_out, NUB, rows, z_cells), f32),
            pltpu.VMEM((n_out, NUB, rows, z_cells), f32),
            pltpu.VMEM((n_out, NUB, rows, z_cells), f32),
            pltpu.VMEM((2 * modes, n_out, MID, per_slab, side), f32),
            pltpu.VMEM((2 * modes, n_out, MID, per_slab, side), f32),
            pltpu.VMEM((n_angle, planes, n_out, MID, per_slab, side), f32),
            pltpu.VMEM((planes, n_out, MID, per_slab, side), f32),
            pltpu.VMEM((planes, n_out, per_slab, side), f32),
            pltpu.VMEM((planes, n_out, per_slab, side), f32),
            pltpu.VMEM((n_out, planes, per_slab, side), f32),
            pltpu.VMEM((n_slab, n_angle, rows, z_cells), f32),
            pltpu.VMEM((n_angle, n_slab, rows, z_cells), f32),
            dma((2,)), dma((2,)),
            dma((n_out,)), dma((n_out,)),
            dma((n_slab,)), dma((n_slab,)),
            dma((n_angle,)), dma((n_angle,)),
            dma((2,)), dma((2,)),
            dma((n_angle,)), dma((n_angle,)),
            dma((n_out,)), dma((n_out,)),
            dma((n_angle,)), dma((n_angle,)),
        ],
        compiler_params=pltpu.CompilerParams(collective_id=1, has_side_effects=True, vmem_limit_bytes=VMEM_BYTES),
    )(
        grad.reshape(n_out, MID, INNER, NUB, rows, z_cells),
        pterm.reshape(2 * modes, n_out, MID, INNER, per_slab, side),
        hot,
    )
    incoming = vin.reshape(n_angle, 2, blk_cols, z_cells)
    tile_grad = jnp.einsum(
        "auk,acuz->ckz", resampling_matrices.astype(f32), incoming, precision=lax.Precision.HIGHEST
    )
    vol_grad = tile_grad.reshape(2, x_cells, y_here, z_cells)
    return (
        vol_grad,
        probe_grad.reshape(modes, 2, per_slab, side),
        resid[None, None],
        shift[None, None],
    )


def solution(mesh):
    in_specs = (
        P(None, "slab", "angle", None),
        P(),
        P(),
        P(),
        P("angle", "slab", None),
        P("angle", "slab", None, None),
    )
    out_specs = (
        P(None, "slab", "angle", None),
        P(None, None, "slab", None),
        P("angle", "slab", None, None),
        P("angle", "slab", None),
    )
    return jax.shard_map(local, mesh=mesh, in_specs=in_specs, out_specs=out_specs, check_vma=False)
```

```python
import functools
import math

import jax
import jax.numpy as jnp
import numpy as np
from jax import lax
from jax.experimental import pallas as pl
from jax.experimental.pallas import tpu as pltpu
from jax.sharding import PartitionSpec as P

NUB = 5
INNER = 2
MID = 2
MESH = pl.DeviceIdType.MESH
VMEM = pl.BlockSpec(memory_space=pltpu.VMEM)
SMEM = pl.BlockSpec(memory_space=pltpu.SMEM)
VMEM_BYTES = 48 * 1024 * 1024


def others(n_slab, n_angle, me_s, me_a, visit):
    for turn in range(1, n_angle + 1):
        step = turn % n_angle
        peer_a = lax.rem(me_a + step, n_angle)

        @pl.loop(1 if step == 0 else 0, n_slab)
        def _(off):
            visit(step, off, {"slab": lax.rem(me_s + off, n_slab), "angle": peer_a})


def greet(n_slab, n_angle, me_s, me_a):
    barrier = pltpu.get_barrier_semaphore()
    others(
        n_slab, n_angle, me_s, me_a,
        lambda step, off, device: pl.semaphore_signal(barrier, inc=1, device_id=device, device_id_type=MESH),
    )
    pl.semaphore_wait(barrier, n_slab * n_angle - 1)


def send(src, dst, send_sem, recv_sem, device):
    return pltpu.make_async_remote_copy(
        src_ref=src, dst_ref=dst, send_sem=send_sem, recv_sem=recv_sem, device_id=device, device_id_type=MESH
    )


def gather_kernel(n_slab, n_angle, blocks, hot, out, got, as_, ar, zs, zr, ys, yr, cs, cr):
    n_out = n_slab // (MID * INNER)
    me_s, me_a = lax.axis_index("slab"), lax.axis_index("angle")
    me_z, me_y, me_c = me_s // (MID * INNER), lax.rem(me_s // INNER, MID), lax.rem(me_s, INNER)
    greet(n_slab, n_angle, me_s, me_a)

    def acopy(step, off, device):
        src = blocks.at[device["angle"], device["slab"]]
        return send(src, got.at[me_a, me_s], as_.at[step, off], ar.at[step, off], device)

    others(n_slab, n_angle, me_s, me_a, lambda *at: acopy(*at).start())
    got[me_a, me_s] = blocks[me_a, me_s]
    others(n_slab, n_angle, me_s, me_a, lambda *at: acopy(*at).wait_recv())

    rows, z_cells = blocks.shape[2], blocks.shape[3]

    def add(i, acc):
        for j in range(n_angle):
            item = got[j, i]
            acc = tuple(acc[d] + hot[(i * n_angle + j) * NUB + d] * item for d in range(NUB))
        return acc

    acc = lax.fori_loop(0, n_slab, add, tuple(jnp.zeros((rows, z_cells), jnp.float32) for _ in range(NUB)))
    for d in range(NUB):
        out[me_z, me_y, me_c, d] = acc[d]

    def to_slab(z, y, c):
        return {"slab": (z * MID + y) * INNER + c}

    def zcopy(off):
        piece = out.at[me_z, me_y, me_c]
        return send(piece, piece, zs.at[off], zr.at[off], to_slab(lax.rem(me_z + off, n_out), me_y, me_c))

    def ycopy(off):
        piece = out.at[lax.rem(me_z + n_out - off, n_out), me_y, me_c]
        return send(piece, piece, ys.at[off], yr.at[off], to_slab(me_z, 1 - me_y, me_c))

    def ccopy(off, flip):
        row = 1 - me_y if flip else me_y
        piece = out.at[lax.rem(me_z + n_out - off, n_out), row, me_c]
        return send(piece, piece, cs.at[flip, off], cr.at[flip, off], to_slab(me_z, me_y, 1 - me_c))

    ycopy(0).start()
    for off in range(1, n_out):
        zcopy(off).start()
    ccopy(0, 0).start()
    for off in range(1, n_out):
        zcopy(off).wait_recv()
        ycopy(off).start()
        ccopy(off, 0).start()
    for off in range(n_out):
        ycopy(off).wait_recv()
        ccopy(off, 1).start()
    for off in range(n_out):
        ccopy(off, 0).wait_recv()
        ccopy(off, 1).wait_recv()
        ycopy(off).wait_send()
        ccopy(off, 0).wait_send()
        ccopy(off, 1).wait_send()
    for off in range(1, n_out):
        zcopy(off).wait_send()
    others(n_slab, n_angle, me_s, me_a, lambda *at: acopy(*at).wait_send())


def split(x):
    high = x.astype(jnp.bfloat16)
    return high, (x - high.astype(jnp.float32)).astype(jnp.bfloat16)


def dot3(a, b):
    def dot(x, y):
        return jnp.dot(x, y, preferred_element_type=jnp.float32)

    return dot(a[0], b[0]) + (dot(a[0], b[1]) + dot(a[1], b[0]))


def adjoint_kernel(
    n_slab, n_angle, far, resid, trans, det, probe, tabs, hot, corner, vin, pr, shift,
    tgrad, pg, p1, s1, p2, s2, p3, disp, q, q1, t1, q2x, t2x, q2y, t2y, q3y, q3x, t3, q4,
    pcs, pcr, pys, pyr, pzs, pzr, ds, dr, qcs, qcr, qxs, qxr, qys, qyr, qzs, qzr, qgs, qgr,
):
    n_out = n_slab // (MID * INNER)
    modes, _, side, _ = probe.shape
    rows, z_cells = disp.shape[2], disp.shape[3]
    per = q.shape[4]
    groups = q1.shape[0]
    me_s, me_a = lax.axis_index("slab"), lax.axis_index("angle")
    me_z, me_y, me_c = me_s // (MID * INNER), lax.rem(me_s // INNER, MID), lax.rem(me_s, INNER)
    greet(n_slab, n_angle, me_s, me_a)

    def to_slab(z, y, c):
        return {"slab": (z * MID + y) * INNER + c}

    core_peer = to_slab(me_z, me_y, 1 - me_c)
    mid_peer = to_slab(me_z, 1 - me_y, me_c)

    def at_z(off):
        return lax.rem(me_z + off, n_out)

    def at_a(off):
        return lax.rem(me_a + off, n_angle)

    def qc(g):
        src = q.at[pl.ds(g * n_angle, n_angle), :, :, 1 - me_c]
        return send(src, q1.at[g], qcs.at[g], qcr.at[g], core_peer)

    def qx(g, off):
        src, dst = (t1.at[g, at_a(off)], q2x.at[g, off]) if g % 2 == 0 else (t2y.at[g, at_a(off)], q3x.at[g, off])
        return send(src, dst, qxs.at[g, off], qxr.at[g, off], {"angle": at_a(off)})

    def qy(g):
        src, dst = (t2x.at[g, :, 1 - me_y], q3y.at[g]) if g % 2 == 0 else (t1.at[g, :, :, 1 - me_y], q2y.at[g])
        return send(src, dst, qys.at[g], qyr.at[g], mid_peer)

    def qz(g, off):
        return send(t3.at[g, at_z(off)], q4.at[g, off], qzs.at[g, off], qzr.at[g, off], to_slab(at_z(off), me_y, me_c))

    def qg(g, off):
        plane = pr.at[g * n_angle + me_a]
        return send(plane, plane, qgs.at[g, off], qgr.at[g, off], {"angle": at_a(off)})

    def start_x(g):
        for off in range(1, n_angle):
            qx(g, off).start()

    def sum_x(g, own, parts):
        total = own
        for off in range(1, n_angle):
            qx(g, off).wait_recv()
            total = total + parts[g, off]
        return total

    def after_core(g):
        qc(g).wait_recv()
        t1[g] = q[g * n_angle : (g + 1) * n_angle, :, :, me_c] + q1[g]
        if g % 2 == 0:
            start_x(g)
        else:
            qy(g).start()

    def after_first(g):
        if g % 2 == 0:
            t2x[g] = sum_x(g, t1[g, me_a], q2x)
            qy(g).start()
        else:
            qy(g).wait_recv()
            t2y[g] = t1[g, :, :, me_y] + q2y[g]
            start_x(g)

    def after_second(g):
        if g % 2 == 0:
            qy(g).wait_recv()
            t3[g] = t2x[g, :, me_y] + q3y[g]
        else:
            t3[g] = sum_x(g, t2y[g, me_a], q3x)
        for off in range(1, n_out):
            qz(g, off).start()

    def after_z(g):
        total = t3[g, me_z]
        for off in range(1, n_out):
            qz(g, off).wait_recv()
            total = total + q4[g, off]
        pr[g * n_angle + me_a] = total
        for off in range(1, n_angle):
            qg(g, off).start()

    left = (tabs[0], tabs[1])
    right = (tabs[2], tabs[3])
    tgrad[...] = jnp.zeros_like(tgrad)
    weight = 2.0 * resid[...]
    for m in range(modes):
        pull = jnp.concatenate([far[m, :, :side] * weight, far[m, :, side:] * weight], axis=0)
        mid = dot3(right, split(pull))
        both = jnp.concatenate([mid[:side], mid[side:]], axis=1)
        back = dot3(split(both), left)
        er, ei = back[:, :side], back[:, side:]
        tr, ti = trans[0], trans[1]
        terms = (er * tr + ei * ti, ei * tr - er * ti)
        for part in range(2):
            for k in range(n_slab):
                z, y, c = k // (MID * INNER), k // INNER % MID, k % INNER
                q[2 * m + part, z, y, c] = terms[part][k * per : (k + 1) * per]
        pr_, pi_ = probe[m, 0].astype(jnp.float32), probe[m, 1].astype(jnp.float32)
        tgrad[0] += pr_ * er + pi_ * ei
        tgrad[1] += pr_ * ei - pi_ * er
        if 2 * (m + 1) % n_angle == 0:
            g = 2 * (m + 1) // n_angle - 1
            qc(g).start()
            if g >= 1:
                after_core(g - 1)
            if g >= 3:
                after_first(g - 3)

    tr, ti = trans[0], trans[1]
    ga, gb = tgrad[0], tgrad[1]
    patch = (gb * tr - ga * ti, -(ga * tr + gb * ti))
    det_cols, lanes = det.shape[1], det.shape[2]
    to_col = (
        lax.broadcasted_iota(jnp.int32, (det_cols, side), 0)
        == lax.broadcasted_iota(jnp.int32, (det_cols, side), 1) + corner[0]
    ).astype(jnp.float32).astype(jnp.bfloat16)
    to_row = (
        lax.broadcasted_iota(jnp.int32, (side, lanes), 0) + corner[1]
        == lax.broadcasted_iota(jnp.int32, (side, lanes), 1)
    ).astype(jnp.float32).astype(jnp.bfloat16)
    per_comp = n_slab // 2
    for c in range(2):
        wide = jnp.dot(to_col, jnp.concatenate(split(patch[c]), axis=1), preferred_element_type=jnp.float32)
        wide = wide.astype(jnp.bfloat16)
        placed = jnp.dot(wide[:, :side], to_row, preferred_element_type=jnp.float32) + jnp.dot(
            wide[:, side:], to_row, preferred_element_type=jnp.float32
        )
        for k in range(c * per_comp, (c + 1) * per_comp):
            z, y, core = k // (MID * INNER), k // INNER % MID, k % INNER
            for d in range(NUB):
                at = (d * per_comp + k % per_comp) * rows
                pg[z, y, core, d] = placed[at : at + rows, :z_cells]

    def pc(off):
        return send(pg.at[at_z(off), :, 1 - me_c], p1.at[off], pcs.at[off], pcr.at[off], core_peer)

    def py(off):
        return send(s1.at[off, 1 - me_y], p2.at[off], pys.at[off], pyr.at[off], mid_peer)

    def pz(off):
        return send(s2.at[off], p3.at[off], pzs.at[off], pzr.at[off], to_slab(at_z(off), me_y, me_c))

    turns = tuple(range(1, n_out)) + (0,)
    for off in turns:
        pc(off).start()
    for off in turns:
        pc(off).wait_recv()
        s1[off] = pg[at_z(off), :, me_c] + p1[off]
        py(off).start()
    after_core(groups - 1)
    for g in range(max(groups - 3, 0), groups - 1):
        after_first(g)
    for c in range(2):
        here = det[c]
        dcol = pltpu.roll(here, det_cols - 1, 0)[:side, :side] - pltpu.roll(here, 1, 0)[:side, :side]
        drow = pltpu.roll(here, lanes - 1, 1)[:side, :side] - pltpu.roll(here, 1, 1)[:side, :side]
        moved = (jnp.sum(patch[c] * dcol) * 0.5 / side, jnp.sum(patch[c] * drow) * 0.5 / side)
        for axis in range(2):
            shift[axis] = moved[axis] if c == 0 else shift[axis] + moved[axis]
    for off in turns:
        py(off).wait_recv()
        s2[off] = s1[off, me_y] + p2[off]
        if off:
            pz(off).start()
    after_first(groups - 1)
    for g in range(groups - 1):
        after_second(g)
    total = s2[0]
    for off in range(1, n_out):
        pz(off).wait_recv()
        total = total + p3[off]

    @pl.loop(0, n_slab)
    def _(i):
        for j in range(n_angle):
            base = (i * n_angle + j) * NUB
            block = hot[base] * total[0]
            for d in range(1, NUB):
                block = block + hot[base + d] * total[d]
            disp[i, j] = block

    def dcopy(step, off, device):
        src = disp.at[device["slab"], device["angle"]]
        return send(src, vin.at[me_a, me_s], ds.at[step, off], dr.at[step, off], device)

    others(n_slab, n_angle, me_s, me_a, lambda *at: dcopy(*at).start())
    vin[me_a, me_s] = disp[me_s, me_a]
    after_second(groups - 1)
    for g in range(groups):
        after_z(g)
    others(n_slab, n_angle, me_s, me_a, lambda *at: dcopy(*at).wait_recv())
    for g in range(groups):
        for off in range(1, n_angle):
            qg(g, off).wait_recv()
            qg(g, off).wait_send()
            qx(g, off).wait_send()
        qc(g).wait_send()
        qy(g).wait_send()
        for off in range(1, n_out):
            qz(g, off).wait_send()
    for off in range(n_out):
        pc(off).wait_send()
        py(off).wait_send()
        if off:
            pz(off).wait_send()
    others(n_slab, n_angle, me_s, me_a, lambda *at: dcopy(*at).wait_send())


def spot_kernel(corner, gathered, probe, power, tabs, inten, far, trans, det):
    n_slab, _, rows, z_cells = gathered.shape
    side = probe.shape[2]
    modes = probe.shape[0]
    det_cols = det.shape[1]
    lanes = det.shape[2]
    per = n_slab // 2
    cols = per * rows
    col, row = corner[0], corner[1]
    for k in range(n_slab):
        for d in range(NUB):
            at = d * cols + (k % per) * rows
            det[k // per, at : at + rows, :z_cells] = gathered[k, d]
    for c in range(2):
        det[c, :, z_cells:] = jnp.zeros((det_cols, lanes - z_cells), jnp.float32)
        moved = pltpu.roll(det[c], lanes - row, 1)
        det[c] = pltpu.roll(moved, det_cols - col, 0)
    absorb = jnp.exp(-det[1, :side, :side])
    phase = det[0, :side, :side]
    trans[0] = absorb * jnp.cos(phase)
    trans[1] = absorb * jnp.sin(phase)
    inten[...] = -power[...]
    left = (tabs[0], tabs[1])
    right = (tabs[2], tabs[3])

    @pl.loop(0, modes)
    def _(m):
        pr_, pi_ = probe[m, 0].astype(jnp.float32), probe[m, 1].astype(jnp.float32)
        tr, ti = trans[0], trans[1]
        stacked = jnp.concatenate([pr_ * tr - pi_ * ti, pr_ * ti + pi_ * tr], axis=0)
        mid = dot3(left, split(stacked))
        both = jnp.concatenate([mid[:side], mid[side:]], axis=1)
        field = dot3(split(both), right)
        far[m] = field
        fr, fi = field[:, :side], field[:, side:]
        inten[...] += fr * fr + fi * fi


def tables(length):
    ids = np.outer(np.arange(length), np.arange(length)) % length
    phases = ids * (2.0 * math.pi / length)
    c, s = np.cos(phases) / math.sqrt(length), np.sin(phases) / math.sqrt(length)
    left = np.block([[c, s], [-s, c]])
    parts = []
    for table in (left, left.T):
        high = table.astype(jnp.bfloat16)
        parts += [high, (table - high.astype(np.float64)).astype(jnp.bfloat16)]
    return jnp.asarray(np.stack(parts))


def local(object_density, resampling_matrices, receiving_tile_number, illumination_modes, window_corners, observed_power):
    n_angle = lax.axis_size("angle")
    n_slab = lax.axis_size("slab")
    n_out = n_slab // (MID * INNER)
    my_angle = lax.axis_index("angle")
    x_cells = object_density.shape[1]
    y_here = object_density.shape[2]
    z_cells = object_density.shape[3]
    tile_rows = resampling_matrices.shape[2]
    blk_cols = resampling_matrices.shape[1]
    modes, _, side, _ = illumination_modes.shape
    rows = 2 * blk_cols // n_slab
    per_slab = side // n_slab
    lanes = (z_cells + 127) // 128 * 128
    f32 = jnp.float32
    dma = pltpu.SemaphoreType.DMA

    tile = object_density.reshape(2, tile_rows, z_cells)
    blocks = jnp.einsum("auk,ckz->acuz", resampling_matrices, tile, preferred_element_type=f32)
    blocks = blocks.reshape(n_angle, n_slab, rows, z_cells)
    ids = lax.dynamic_index_in_dim(receiving_tile_number, my_angle, 0, keepdims=False).reshape(-1)
    hot = (ids[:, None] == jnp.arange(NUB, dtype=jnp.int32)[None, :]).astype(f32).reshape(-1)

    gathered = pl.pallas_call(
        functools.partial(gather_kernel, n_slab, n_angle),
        out_shape=jax.ShapeDtypeStruct((n_out, MID, INNER, NUB, rows, z_cells), f32),
        in_specs=[VMEM, SMEM],
        out_specs=VMEM,
        scratch_shapes=[
            pltpu.VMEM((n_angle, n_slab, rows, z_cells), f32),
            dma((n_angle, n_slab)), dma((n_angle, n_slab)),
            dma((n_out,)), dma((n_out,)),
            dma((n_out,)), dma((n_out,)),
            dma((2, n_out)), dma((2, n_out)),
        ],
        compiler_params=pltpu.CompilerParams(collective_id=0, has_side_effects=True, vmem_limit_bytes=VMEM_BYTES),
    )(blocks, hot)

    tabs = tables(side)
    corner = window_corners.reshape(2)
    resid, far, trans, det = pl.pallas_call(
        spot_kernel,
        out_shape=(
            jax.ShapeDtypeStruct((side, side), f32),
            jax.ShapeDtypeStruct((modes, side, 2 * side), f32),
            jax.ShapeDtypeStruct((2, side, side), f32),
            jax.ShapeDtypeStruct((2, blk_cols * NUB, lanes), f32),
        ),
        in_specs=[SMEM, VMEM, VMEM, VMEM, VMEM],
        out_specs=(VMEM, VMEM, VMEM, VMEM),
        compiler_params=pltpu.CompilerParams(vmem_limit_bytes=VMEM_BYTES),
    )(corner, gathered.reshape(n_slab, NUB, rows, z_cells), illumination_modes, observed_power[0, 0], tabs)

    groups = 2 * modes // n_angle
    shapes = (
        (2, side, side),
        (n_out, MID, INNER, NUB, rows, z_cells),
        (n_out, MID, NUB, rows, z_cells),
        (n_out, MID, NUB, rows, z_cells),
        (n_out, NUB, rows, z_cells),
        (n_out, NUB, rows, z_cells),
        (n_out, NUB, rows, z_cells),
        (n_slab, n_angle, rows, z_cells),
        (2 * modes, n_out, MID, INNER, per_slab, side),
        (groups, n_angle, n_out, MID, per_slab, side),
        (groups, n_angle, n_out, MID, per_slab, side),
        (groups, n_angle, n_out, MID, per_slab, side),
        (groups, n_out, MID, per_slab, side),
        (groups, n_angle, n_out, per_slab, side),
        (groups, n_angle, n_out, per_slab, side),
        (groups, n_out, per_slab, side),
        (groups, n_angle, n_out, per_slab, side),
        (groups, n_out, per_slab, side),
        (groups, n_out, per_slab, side),
    )
    sems = (
        (n_out,), (n_out,), (n_out,), (n_angle, n_slab),
        (groups,), (groups, n_angle), (groups,), (groups, n_out), (groups, n_angle),
    )
    vin, probe_grad, shift = pl.pallas_call(
        functools.partial(adjoint_kernel, n_slab, n_angle),
        out_shape=(
            jax.ShapeDtypeStruct((n_angle, n_slab, rows, z_cells), f32),
            jax.ShapeDtypeStruct((2 * modes, per_slab, side), f32),
            jax.ShapeDtypeStruct((2,), f32),
        ),
        in_specs=[VMEM] * 6 + [SMEM, SMEM],
        out_specs=(VMEM, VMEM, SMEM),
        scratch_shapes=[pltpu.VMEM(shape, f32) for shape in shapes] + [dma(shape) for shape in sems for _ in range(2)],
        compiler_params=pltpu.CompilerParams(collective_id=1, has_side_effects=True, vmem_limit_bytes=VMEM_BYTES),
    )(far, resid, trans, det, illumination_modes, tabs, hot, corner)
    incoming = vin.reshape(n_angle, 2, blk_cols, z_cells)
    tile_grad = jnp.einsum(
        "auk,acuz->ckz", resampling_matrices.astype(f32), incoming, precision=lax.Precision.HIGHEST
    )
    vol_grad = tile_grad.reshape(2, x_cells, y_here, z_cells)
    return (
        vol_grad,
        probe_grad.reshape(modes, 2, per_slab, side),
        resid[None, None],
        shift[None, None],
    )


def solution(mesh):
    in_specs = (
        P(None, "slab", "angle", None),
        P(),
        P(),
        P(),
        P("angle", "slab", None),
        P("angle", "slab", None, None),
    )
    out_specs = (
        P(None, "slab", "angle", None),
        P(None, None, "slab", None),
        P("angle", "slab", None, None),
        P("angle", "slab", None),
    )
    return jax.shard_map(local, mesh=mesh, in_specs=in_specs, out_specs=out_specs, check_vma=False)
```

```python
import functools
import math

import jax
import jax.numpy as jnp
import numpy as np
from jax import lax
from jax.experimental import pallas as pl
from jax.experimental.pallas import tpu as pltpu
from jax.sharding import PartitionSpec as P

NUB = 5
INNER = 2
MID = 2
MESH = pl.DeviceIdType.MESH
VMEM = pl.BlockSpec(memory_space=pltpu.VMEM)
SMEM = pl.BlockSpec(memory_space=pltpu.SMEM)
VMEM_BYTES = 32 * 1024 * 1024


def others(n_slab, n_angle, me_s, me_a, visit):
    for turn in range(1, n_angle + 1):
        step = turn % n_angle
        peer_a = lax.rem(me_a + step, n_angle)

        @pl.loop(1 if step == 0 else 0, n_slab)
        def _(off):
            visit(step, off, {"slab": lax.rem(me_s + off, n_slab), "angle": peer_a})


def greet(n_slab, n_angle, me_s, me_a):
    barrier = pltpu.get_barrier_semaphore()
    others(
        n_slab, n_angle, me_s, me_a,
        lambda step, off, device: pl.semaphore_signal(barrier, inc=1, device_id=device, device_id_type=MESH),
    )
    pl.semaphore_wait(barrier, n_slab * n_angle - 1)


def send(src, dst, send_sem, recv_sem, device):
    return pltpu.make_async_remote_copy(
        src_ref=src, dst_ref=dst, send_sem=send_sem, recv_sem=recv_sem, device_id=device, device_id_type=MESH
    )


def gather_kernel(n_slab, n_angle, blocks, hot, out, got, as_, ar, zs, zr, ys, yr, cs, cr):
    n_out = n_slab // (MID * INNER)
    me_s, me_a = lax.axis_index("slab"), lax.axis_index("angle")
    me_z, me_y, me_c = me_s // (MID * INNER), lax.rem(me_s // INNER, MID), lax.rem(me_s, INNER)
    greet(n_slab, n_angle, me_s, me_a)

    def acopy(step, off, device):
        src = blocks.at[device["angle"], device["slab"]]
        return send(src, got.at[me_a, me_s], as_.at[step, off], ar.at[step, off], device)

    others(n_slab, n_angle, me_s, me_a, lambda *at: acopy(*at).start())
    got[me_a, me_s] = blocks[me_a, me_s]
    others(n_slab, n_angle, me_s, me_a, lambda *at: acopy(*at).wait_recv())

    rows, z_cells = blocks.shape[2], blocks.shape[3]

    def add(i, acc):
        for j in range(n_angle):
            item = got[j, i]
            acc = tuple(acc[d] + hot[(i * n_angle + j) * NUB + d] * item for d in range(NUB))
        return acc

    acc = lax.fori_loop(0, n_slab, add, tuple(jnp.zeros((rows, z_cells), jnp.float32) for _ in range(NUB)))
    for d in range(NUB):
        out[me_z, me_y, me_c, d] = acc[d]

    def to_slab(z, y, c):
        return {"slab": (z * MID + y) * INNER + c}

    def zcopy(off):
        piece = out.at[me_z, me_y, me_c]
        return send(piece, piece, zs.at[off], zr.at[off], to_slab(lax.rem(me_z + off, n_out), me_y, me_c))

    def ycopy(off):
        piece = out.at[lax.rem(me_z + n_out - off, n_out), me_y, me_c]
        return send(piece, piece, ys.at[off], yr.at[off], to_slab(me_z, 1 - me_y, me_c))

    def ccopy(off, flip):
        row = 1 - me_y if flip else me_y
        piece = out.at[lax.rem(me_z + n_out - off, n_out), row, me_c]
        return send(piece, piece, cs.at[flip, off], cr.at[flip, off], to_slab(me_z, me_y, 1 - me_c))

    ycopy(0).start()
    for off in range(1, n_out):
        zcopy(off).start()
    ccopy(0, 0).start()
    for off in range(1, n_out):
        zcopy(off).wait_recv()
        ycopy(off).start()
        ccopy(off, 0).start()
    for off in range(n_out):
        ycopy(off).wait_recv()
        ccopy(off, 1).start()
    for off in range(n_out):
        ccopy(off, 0).wait_recv()
        ccopy(off, 1).wait_recv()
        ycopy(off).wait_send()
        ccopy(off, 0).wait_send()
        ccopy(off, 1).wait_send()
    for off in range(1, n_out):
        zcopy(off).wait_send()
    others(n_slab, n_angle, me_s, me_a, lambda *at: acopy(*at).wait_send())


def block_tables(tabs):
    left, right = [], []
    for part in range(2):
        c, s = tabs[part], tabs[2 + part]
        plus, minus = jnp.concatenate([c, s], axis=1), jnp.concatenate([-s, c], axis=1)
        left.append(jnp.concatenate([plus, minus], axis=0))
        plus, minus = jnp.concatenate([c, -s], axis=1), jnp.concatenate([s, c], axis=1)
        right.append(jnp.concatenate([plus, minus], axis=0))
    return left, right


def split(x):
    high = x.astype(jnp.bfloat16)
    return high, (x - high.astype(jnp.float32)).astype(jnp.bfloat16)


def dot3(a, b):
    def dot(x, y):
        return jnp.dot(x, y, preferred_element_type=jnp.float32)

    return dot(a[0], b[0]) + (dot(a[0], b[1]) + dot(a[1], b[0]))


def adjoint_kernel(
    n_slab, n_angle, far, resid, trans, det, probe, tabs, hot, corner, vin, pr, shift,
    tgrad, pg, p1, s1, p2, s2, p3, disp, q, q1, t1, q2x, t2x, q2y, t2y, q3y, q3x, t3, q4, t4, q5,
    pcs, pcr, pys, pyr, pzs, pzr, ds, dr, qcs, qcr, qxs, qxr, qys, qyr, qzs, qzr, qhs, qhr, qgs, qgr,
):
    n_out = n_slab // (MID * INNER)
    modes, _, side, _ = probe.shape
    rows, z_cells = disp.shape[2], disp.shape[3]
    per = q.shape[4]
    groups = q1.shape[0]
    me_s, me_a = lax.axis_index("slab"), lax.axis_index("angle")
    me_z, me_y, me_c = me_s // (MID * INNER), lax.rem(me_s // INNER, MID), lax.rem(me_s, INNER)
    greet(n_slab, n_angle, me_s, me_a)

    def to_slab(z, y, c):
        return {"slab": (z * MID + y) * INNER + c}

    core_peer = to_slab(me_z, me_y, 1 - me_c)
    mid_peer = to_slab(me_z, 1 - me_y, me_c)

    def at_z(off):
        return lax.rem(me_z + off, n_out)

    def at_a(off):
        return lax.rem(me_a + off, n_angle)

    def qc(g):
        src = q.at[pl.ds(g * n_angle, n_angle), :, :, 1 - me_c]
        return send(src, q1.at[g], qcs.at[g], qcr.at[g], core_peer)

    def qx(g, off):
        src, dst = (t1.at[g, at_a(off)], q2x.at[g, off]) if g % 2 == 0 else (t2y.at[g, at_a(off)], q3x.at[g, off])
        return send(src, dst, qxs.at[g, off], qxr.at[g, off], {"angle": at_a(off)})

    def qy(g):
        src, dst = (t2x.at[g, :, 1 - me_y], q3y.at[g]) if g % 2 == 0 else (t1.at[g, :, :, 1 - me_y], q2y.at[g])
        return send(src, dst, qys.at[g], qyr.at[g], mid_peer)

    n_half = n_out // 2
    me_high, me_low = me_z // 2, lax.rem(me_z, 2)

    def at_high(off):
        return lax.rem(me_high + off, n_half)

    def qz(g):
        peer = to_slab(me_high * 2 + 1 - me_low, me_y, me_c)
        return send(t3.at[g, :, 1 - me_low], q4.at[g], qzs.at[g], qzr.at[g], peer)

    def qh(g, off):
        peer = to_slab(at_high(off) * 2 + me_low, me_y, me_c)
        return send(t4.at[g, at_high(off)], q5.at[g, off], qhs.at[g, off], qhr.at[g, off], peer)

    def qg(g, off):
        plane = pr.at[g * n_angle + me_a]
        return send(plane, plane, qgs.at[g, off], qgr.at[g, off], {"angle": at_a(off)})

    def start_x(g):
        for off in range(1, n_angle):
            qx(g, off).start()

    def sum_x(g, own, parts):
        total = own
        for off in range(1, n_angle):
            qx(g, off).wait_recv()
            total = total + parts[g, off]
        return total

    def after_core(g):
        qc(g).wait_recv()
        t1[g] = q[g * n_angle : (g + 1) * n_angle, :, :, me_c] + q1[g]
        if g % 2 == 0:
            start_x(g)
        else:
            qy(g).start()

    def after_first(g):
        if g % 2 == 0:
            t2x[g] = sum_x(g, t1[g, me_a], q2x)
            qy(g).start()
        else:
            qy(g).wait_recv()
            t2y[g] = t1[g, :, :, me_y] + q2y[g]
            start_x(g)

    def after_second(g):
        if g % 2 == 0:
            qy(g).wait_recv()
            total = t2x[g, :, me_y] + q3y[g]
        else:
            total = sum_x(g, t2y[g, me_a], q3x)
        for z in range(n_out):
            t3[g, z // 2, z % 2] = total[z]
        qz(g).start()

    def after_near(g):
        qz(g).wait_recv()
        t4[g] = t3[g, :, me_low] + q4[g]
        for off in range(1, n_half):
            qh(g, off).start()

    def after_z(g):
        total = t4[g, me_high]
        for off in range(1, n_half):
            qh(g, off).wait_recv()
            total = total + q5[g, off]
        pr[g * n_angle + me_a] = total
        for off in range(1, n_angle):
            qg(g, off).start()

    left, right = block_tables(tabs)
    tgrad[...] = jnp.zeros_like(tgrad)
    weight = 2.0 * resid[...]
    for m in range(modes):
        pull = jnp.concatenate([far[m, :, :side] * weight, far[m, :, side:] * weight], axis=0)
        mid = dot3(right, split(pull))
        both = jnp.concatenate([mid[:side], mid[side:]], axis=1)
        back = dot3(split(both), left)
        er, ei = back[:, :side], back[:, side:]
        tr, ti = trans[0], trans[1]
        terms = (er * tr + ei * ti, ei * tr - er * ti)
        for part in range(2):
            for k in range(n_slab):
                z, y, c = k // (MID * INNER), k // INNER % MID, k % INNER
                q[2 * m + part, z, y, c] = terms[part][k * per : (k + 1) * per]
        pr_, pi_ = probe[m, 0].astype(jnp.float32), probe[m, 1].astype(jnp.float32)
        tgrad[0] += pr_ * er + pi_ * ei
        tgrad[1] += pr_ * ei - pi_ * er
        if 2 * (m + 1) % n_angle == 0:
            g = 2 * (m + 1) // n_angle - 1
            qc(g).start()
            if g >= 1:
                after_core(g - 1)
            if g >= 3:
                after_first(g - 3)

    tr, ti = trans[0], trans[1]
    ga, gb = tgrad[0], tgrad[1]
    patch = (gb * tr - ga * ti, -(ga * tr + gb * ti))
    det_cols, lanes = det.shape[1], det.shape[2]
    to_col = (
        lax.broadcasted_iota(jnp.int32, (det_cols, side), 0)
        == lax.broadcasted_iota(jnp.int32, (det_cols, side), 1) + corner[0]
    ).astype(jnp.float32).astype(jnp.bfloat16)
    to_row = (
        lax.broadcasted_iota(jnp.int32, (side, lanes), 0) + corner[1]
        == lax.broadcasted_iota(jnp.int32, (side, lanes), 1)
    ).astype(jnp.float32).astype(jnp.bfloat16)
    per_comp = n_slab // 2
    for c in range(2):
        wide = jnp.dot(to_col, jnp.concatenate(split(patch[c]), axis=1), preferred_element_type=jnp.float32)
        wide = wide.astype(jnp.bfloat16)
        placed = jnp.dot(wide[:, :side], to_row, preferred_element_type=jnp.float32) + jnp.dot(
            wide[:, side:], to_row, preferred_element_type=jnp.float32
        )
        for k in range(c * per_comp, (c + 1) * per_comp):
            z, y, core = k // (MID * INNER), k // INNER % MID, k % INNER
            for d in range(NUB):
                at = (d * per_comp + k % per_comp) * rows
                pg[z, y, core, d] = placed[at : at + rows, :z_cells]

    def pc(off):
        return send(pg.at[at_z(off), :, 1 - me_c], p1.at[off], pcs.at[off], pcr.at[off], core_peer)

    def py(off):
        return send(s1.at[off, 1 - me_y], p2.at[off], pys.at[off], pyr.at[off], mid_peer)

    def pz(off):
        return send(s2.at[off], p3.at[off], pzs.at[off], pzr.at[off], to_slab(at_z(off), me_y, me_c))

    turns = tuple(range(1, n_out)) + (0,)
    for off in turns:
        pc(off).start()
    for off in turns:
        pc(off).wait_recv()
        s1[off] = pg[at_z(off), :, me_c] + p1[off]
        py(off).start()
    after_core(groups - 1)
    for g in range(max(groups - 3, 0), groups - 1):
        after_first(g)
    for c in range(2):
        here = det[c]
        dcol = pltpu.roll(here, det_cols - 1, 0)[:side, :side] - pltpu.roll(here, 1, 0)[:side, :side]
        drow = pltpu.roll(here, lanes - 1, 1)[:side, :side] - pltpu.roll(here, 1, 1)[:side, :side]
        moved = (jnp.sum(patch[c] * dcol) * 0.5 / side, jnp.sum(patch[c] * drow) * 0.5 / side)
        for axis in range(2):
            shift[axis] = moved[axis] if c == 0 else shift[axis] + moved[axis]
    for off in turns:
        py(off).wait_recv()
        s2[off] = s1[off, me_y] + p2[off]
        if off:
            pz(off).start()
    after_first(groups - 1)
    for g in range(groups - 1):
        after_second(g)
    total = s2[0]
    for off in range(1, n_out):
        pz(off).wait_recv()
        total = total + p3[off]

    @pl.loop(0, n_slab)
    def _(i):
        for j in range(n_angle):
            base = (i * n_angle + j) * NUB
            block = hot[base] * total[0]
            for d in range(1, NUB):
                block = block + hot[base + d] * total[d]
            disp[i, j] = block

    def dcopy(step, off, device):
        src = disp.at[device["slab"], device["angle"]]
        return send(src, vin.at[me_a, me_s], ds.at[step, off], dr.at[step, off], device)

    others(n_slab, n_angle, me_s, me_a, lambda *at: dcopy(*at).start())
    vin[me_a, me_s] = disp[me_s, me_a]
    after_second(groups - 1)
    for g in range(groups):
        after_near(g)
    for g in range(groups):
        after_z(g)
    others(n_slab, n_angle, me_s, me_a, lambda *at: dcopy(*at).wait_recv())
    for g in range(groups):
        for off in range(1, n_angle):
            qg(g, off).wait_recv()
            qg(g, off).wait_send()
            qx(g, off).wait_send()
        qc(g).wait_send()
        qy(g).wait_send()
        qz(g).wait_send()
        for off in range(1, n_half):
            qh(g, off).wait_send()
    for off in range(n_out):
        pc(off).wait_send()
        py(off).wait_send()
        if off:
            pz(off).wait_send()
    others(n_slab, n_angle, me_s, me_a, lambda *at: dcopy(*at).wait_send())


def spot_kernel(corner, gathered, probe, power, tabs, inten, far, trans, det):
    n_slab, _, rows, z_cells = gathered.shape
    side = probe.shape[2]
    modes = probe.shape[0]
    det_cols = det.shape[1]
    lanes = det.shape[2]
    per = n_slab // 2
    cols = per * rows
    col, row = corner[0], corner[1]
    for k in range(n_slab):
        for d in range(NUB):
            at = d * cols + (k % per) * rows
            det[k // per, at : at + rows, :z_cells] = gathered[k, d]
    for c in range(2):
        det[c, :, z_cells:] = jnp.zeros((det_cols, lanes - z_cells), jnp.float32)
        moved = pltpu.roll(det[c], lanes - row, 1)
        det[c] = pltpu.roll(moved, det_cols - col, 0)
    absorb = jnp.exp(-det[1, :side, :side])
    phase = det[0, :side, :side]
    trans[0] = absorb * jnp.cos(phase)
    trans[1] = absorb * jnp.sin(phase)
    inten[...] = -power[...]
    left, right = block_tables(tabs)

    @pl.loop(0, modes)
    def _(m):
        pr_, pi_ = probe[m, 0].astype(jnp.float32), probe[m, 1].astype(jnp.float32)
        tr, ti = trans[0], trans[1]
        stacked = jnp.concatenate([pr_ * tr - pi_ * ti, pr_ * ti + pi_ * tr], axis=0)
        mid = dot3(left, split(stacked))
        both = jnp.concatenate([mid[:side], mid[side:]], axis=1)
        field = dot3(split(both), right)
        far[m] = field
        fr, fi = field[:, :side], field[:, side:]
        inten[...] += fr * fr + fi * fi


def spread_kernel(weights, incoming, out):
    n_angle = incoming.shape[0]
    for c in range(2):
        high, low = split(jnp.concatenate([incoming[a, c] for a in range(n_angle)], axis=0))
        out[c] = jnp.dot(weights[...], high, preferred_element_type=jnp.float32) + jnp.dot(
            weights[...], low, preferred_element_type=jnp.float32
        )


def tables(length):
    ids = np.outer(np.arange(length), np.arange(length)) % length
    phases = ids * (2.0 * math.pi / length)
    parts = []
    for table in (np.cos(phases) / math.sqrt(length), np.sin(phases) / math.sqrt(length)):
        high = table.astype(jnp.bfloat16)
        parts += [high, (table - high.astype(np.float64)).astype(jnp.bfloat16)]
    return jnp.asarray(np.stack(parts))


def local(object_density, resampling_matrices, receiving_tile_number, illumination_modes, window_corners, observed_power):
    n_angle = lax.axis_size("angle")
    n_slab = lax.axis_size("slab")
    n_out = n_slab // (MID * INNER)
    my_angle = lax.axis_index("angle")
    x_cells = object_density.shape[1]
    y_here = object_density.shape[2]
    z_cells = object_density.shape[3]
    tile_rows = resampling_matrices.shape[2]
    blk_cols = resampling_matrices.shape[1]
    modes, _, side, _ = illumination_modes.shape
    rows = 2 * blk_cols // n_slab
    per_slab = side // n_slab
    lanes = (z_cells + 127) // 128 * 128
    f32 = jnp.float32
    dma = pltpu.SemaphoreType.DMA

    tile = object_density.reshape(2, tile_rows, z_cells)
    blocks = jnp.einsum("auk,ckz->acuz", resampling_matrices, tile, preferred_element_type=f32)
    blocks = blocks.reshape(n_angle, n_slab, rows, z_cells)
    ids = lax.dynamic_index_in_dim(receiving_tile_number, my_angle, 0, keepdims=False).reshape(-1)
    hot = (ids[:, None] == jnp.arange(NUB, dtype=jnp.int32)[None, :]).astype(f32).reshape(-1)

    gathered = pl.pallas_call(
        functools.partial(gather_kernel, n_slab, n_angle),
        out_shape=jax.ShapeDtypeStruct((n_out, MID, INNER, NUB, rows, z_cells), f32),
        in_specs=[VMEM, SMEM],
        out_specs=VMEM,
        scratch_shapes=[
            pltpu.VMEM((n_angle, n_slab, rows, z_cells), f32),
            dma((n_angle, n_slab)), dma((n_angle, n_slab)),
            dma((n_out,)), dma((n_out,)),
            dma((n_out,)), dma((n_out,)),
            dma((2, n_out)), dma((2, n_out)),
        ],
        compiler_params=pltpu.CompilerParams(collective_id=0, has_side_effects=True, vmem_limit_bytes=VMEM_BYTES),
    )(blocks, hot)

    tabs = tables(side)
    corner = window_corners.reshape(2)
    resid, far, trans, det = pl.pallas_call(
        spot_kernel,
        out_shape=(
            jax.ShapeDtypeStruct((side, side), f32),
            jax.ShapeDtypeStruct((modes, side, 2 * side), f32),
            jax.ShapeDtypeStruct((2, side, side), f32),
            jax.ShapeDtypeStruct((2, blk_cols * NUB, lanes), f32),
        ),
        in_specs=[SMEM, VMEM, VMEM, VMEM, VMEM],
        out_specs=(VMEM, VMEM, VMEM, VMEM),
        compiler_params=pltpu.CompilerParams(vmem_limit_bytes=VMEM_BYTES),
    )(corner, gathered.reshape(n_slab, NUB, rows, z_cells), illumination_modes, observed_power[0, 0], tabs)

    groups = 2 * modes // n_angle
    shapes = (
        (2, side, side),
        (n_out, MID, INNER, NUB, rows, z_cells),
        (n_out, MID, NUB, rows, z_cells),
        (n_out, MID, NUB, rows, z_cells),
        (n_out, NUB, rows, z_cells),
        (n_out, NUB, rows, z_cells),
        (n_out, NUB, rows, z_cells),
        (n_slab, n_angle, rows, z_cells),
        (2 * modes, n_out, MID, INNER, per_slab, side),
        (groups, n_angle, n_out, MID, per_slab, side),
        (groups, n_angle, n_out, MID, per_slab, side),
        (groups, n_angle, n_out, MID, per_slab, side),
        (groups, n_out, MID, per_slab, side),
        (groups, n_angle, n_out, per_slab, side),
        (groups, n_angle, n_out, per_slab, side),
        (groups, n_out, per_slab, side),
        (groups, n_angle, n_out, per_slab, side),
        (groups, n_out // 2, 2, per_slab, side),
        (groups, n_out // 2, per_slab, side),
        (groups, n_out // 2, per_slab, side),
        (groups, n_out // 2, per_slab, side),
    )
    sems = (
        (n_out,), (n_out,), (n_out,), (n_angle, n_slab),
        (groups,), (groups, n_angle), (groups,), (groups,), (groups, n_out // 2), (groups, n_angle),
    )
    vin, probe_grad, shift = pl.pallas_call(
        functools.partial(adjoint_kernel, n_slab, n_angle),
        out_shape=(
            jax.ShapeDtypeStruct((n_angle, n_slab, rows, z_cells), f32),
            jax.ShapeDtypeStruct((2 * modes, per_slab, side), f32),
            jax.ShapeDtypeStruct((2,), f32),
        ),
        in_specs=[VMEM] * 6 + [SMEM, SMEM],
        out_specs=(VMEM, VMEM, SMEM),
        scratch_shapes=[pltpu.VMEM(shape, f32) for shape in shapes] + [dma(shape) for shape in sems for _ in range(2)],
        compiler_params=pltpu.CompilerParams(collective_id=1, has_side_effects=True, vmem_limit_bytes=VMEM_BYTES),
    )(far, resid, trans, det, illumination_modes, tabs, hot, corner)
    tile_grad = pl.pallas_call(
        spread_kernel,
        out_shape=jax.ShapeDtypeStruct((2, tile_rows, z_cells), f32),
        in_specs=[VMEM, VMEM],
        out_specs=VMEM,
        compiler_params=pltpu.CompilerParams(vmem_limit_bytes=VMEM_BYTES),
    )(
        resampling_matrices.reshape(n_angle * blk_cols, tile_rows).T,
        vin.reshape(n_angle, 2, blk_cols, z_cells),
    )
    vol_grad = tile_grad.reshape(2, x_cells, y_here, z_cells)
    return (
        vol_grad,
        probe_grad.reshape(modes, 2, per_slab, side),
        resid[None, None],
        shift[None, None],
    )


def solution(mesh):
    in_specs = (
        P(None, "slab", "angle", None),
        P(),
        P(),
        P(),
        P("angle", "slab", None),
        P("angle", "slab", None, None),
    )
    out_specs = (
        P(None, "slab", "angle", None),
        P(None, None, "slab", None),
        P("angle", "slab", None, None),
        P("angle", "slab", None),
    )
    return jax.shard_map(local, mesh=mesh, in_specs=in_specs, out_specs=out_specs, check_vma=False)
```
